32 devices in a mesh: groups: 2 (over x), row: 16 (over z, y, core).
Axes of the slice: x: 2, y: 2, z: 4, core: 2. Of those that a mesh axis runs over, the one named last changes fastest.
Arguments:
- features: bfloat16 [64, 256, 512], P(('groups', 'row')), parts along dimension 0, may hold values from -6 to 6
- labels: int32 [64, 256], P(('groups', 'row')), parts along dimension 0, may hold values from 0 to 7
- kernel_one: bfloat16 [3, 3, 512, 512], replicated, may hold values from -0.09375 to 0.09375
- kernel_two: bfloat16 [3, 3, 512, 512], replicated, may hold values from -0.09375 to 0.09375
- head_weight: bfloat16 [512, 8], replicated, may hold values from -1 to 1
Outputs:
- section_out: bfloat16 [64, 256, 512], P(('groups', 'row')), parts along dimension 0
- grad_one: float32 [1024, 3, 3, 512], P(('groups', 'row')), parts along dimension 0
- grad_two: float32 [1024, 3, 3, 512], P(('groups', 'row')), parts along dimension 0
- grad_head: float32 [1024, 8], P(('groups', 'row')), parts along dimension 0
The draws below stay inside these ranges and needn't reach their ends.
There are 2 independent parts, one for each index of `groups`. The reference program is written for one: setup_inputs(seed, part) draws one part's arguments, and reference() takes and returns one part's arrays. A program takes and returns all parts, laid end to end along the dimension named above; an argument that names none is the same for every part. Nothing has to cross between parts.
All inputs are finite; a program needn't handle non-finite values.
Results may differ from the reference program's by a relative error of at most 0.019.
The reference program's roundings to bfloat16 on the way (of `hidden`, `dlogits`, `dout` and `dhidden`) count: a program that leaves them out, or rounds other values in their place, can miss the bound.
Values may be sent and summed in bfloat16 or wider, within the bound.
A program may use at most 128 MiB of HBM per device.

```python
import math
import jax
import jax.numpy as jnp
from jax import lax

C = 512
NCLASS = 8
COLS = 256
HEIGHT = 32


def draw_head_weight(key, part):
    key = jax.random.fold_in(key, 11)
    raw = jax.random.truncated_normal(key, -3.0, 3.0, (C, NCLASS), jnp.float32)
    centred = raw - jnp.mean(raw, axis=1, keepdims=True)
    return (centred * (0.03 / math.sqrt(C))).astype(jnp.bfloat16)


def set_ends(entries, rng, smallest, top_value):
    extent = entries.shape
    spot = [jax.random.randint(jax.random.fold_in(rng, axis), (), 0, extent[axis]) for axis in range(len(extent))]
    entries = entries.at[tuple(spot)].set(smallest)
    longest = extent.index(max(extent))
    spot[longest] = (spot[longest] + 1) % extent[longest]
    return entries.at[tuple(spot)].set(top_value)


def spiked(entries, rng, source, target, blocks, factor):
    def block_of(dim):
        return (jnp.arange(entries.shape[dim]) // (entries.shape[dim] // blocks)).reshape((-1,) + (1,) * (entries.ndim - 1 - dim))

    first = jax.random.permutation(rng, blocks)[block_of(target)]
    second = (block_of(target) + blocks // 2) % blocks
    return jnp.where((block_of(source) == first) | (block_of(source) == second), factor * entries, entries)


def block_levels(rng, dims, shards, smallest, top_value):
    level, own = 1.0, jax.random.fold_in(rng, 6)
    for axis_at, blocks in shards:
        draws = jnp.exp(jax.random.uniform(jax.random.fold_in(own, axis_at), (blocks,), jnp.float32, smallest / len(shards), top_value / len(shards)))
        level = level * jnp.repeat(draws, dims[axis_at] // blocks).reshape([-1 if axis == axis_at else 1 for axis in range(len(dims))])
    return level


def normal_values(key, dims, scale, limit, split=(), kind=jnp.bfloat16):
    result = scale * jax.random.normal(key, dims, jnp.float32)
    if split:
        result = result * block_levels(key, dims, split, -0.22, 0.18)
    return jnp.clip(result, -limit, limit).astype(kind)


def heavy_noise(stream_key, dims, spread, reach, cuts, heavy, held_as=jnp.bfloat16):
    entries = spread * jax.random.normal(stream_key, dims, jnp.float32)
    if cuts:
        entries = entries * block_levels(stream_key, dims, cuts, -0.22, 0.18)
    return jnp.clip(spiked(entries, jax.random.fold_in(stream_key, 3), *heavy), -reach, reach).astype(held_as)


def setup_inputs(seed: int = 0, part: int = 0) -> dict:
    key_list = jax.random.split(jax.random.key(seed), 6)
    part_keys = jax.random.split(jax.random.fold_in(key_list[5], part), 6)
    features = heavy_noise(part_keys[0], (HEIGHT, COLS, C), 1.0, 6.0, ((0, 16),), (0, 2, 16, 2.0))
    labels = set_ends(jax.random.randint(part_keys[1], (HEIGHT, COLS), 0, NCLASS), jax.random.fold_in(part_keys[1], 1), 0, NCLASS - 1).astype(jnp.int32)
    kernel_one = normal_values(key_list[2], (3, 3, C, C), (9 * C) ** -0.5, 0.09375)
    kernel_two = normal_values(key_list[3], (3, 3, C, C), (9 * C) ** -0.5, 0.09375)
    head_weight = draw_head_weight(jax.random.fold_in(key_list[5], 71), part)
    return {"features": features, "labels": labels, "kernel_one": kernel_one, "kernel_two": kernel_two, "head_weight": head_weight}


def shifted(padded, row_off, col_off, height, width):
    return padded[row_off:row_off + height, col_off:col_off + width].reshape(height * width, -1).astype(jnp.float32)

def convolve(values, kernel):
    height, width, chans = values.shape
    padded = jnp.pad(values, ((1, 1), (1, 1), (0, 0)))
    kernel_f = kernel.astype(jnp.float32)
    total = jnp.zeros((height * width, kernel.shape[3]), jnp.float32)
    for tap_a in range(3):
        for tap_b in range(3):
            total = total + jnp.dot(shifted(padded, tap_a, tap_b, height, width), kernel_f[tap_a, tap_b], precision=lax.Precision.HIGHEST)
    return total.reshape(height, width, -1)

def kernel_grad(values, cotan):
    height, width, chans = values.shape
    padded = jnp.pad(values, ((1, 1), (1, 1), (0, 0)))
    cot_flat = cotan.reshape(height * width, -1).astype(jnp.float32)
    blocks = []
    for tap_a in range(3):
        for tap_b in range(3):
            blocks.append(jnp.dot(shifted(padded, tap_a, tap_b, height, width).T, cot_flat, precision=lax.Precision.HIGHEST))
    stacked = jnp.stack(blocks, axis=1)
    return stacked.reshape(chans, 3, 3, -1)

def reference(features, labels, kernel_one, kernel_two, head_weight):
    height, width, chans = features.shape
    hidden = jnp.maximum(convolve(features, kernel_one), 0.0).astype(jnp.bfloat16)
    section_out = jnp.maximum(convolve(hidden, kernel_two), 0.0).astype(jnp.bfloat16)
    flat_out = section_out.reshape(height * width, chans).astype(jnp.float32)
    head_f = head_weight.astype(jnp.float32)
    logits = jnp.dot(flat_out, head_f, precision=lax.Precision.HIGHEST)
    onehot = (labels.reshape(-1)[:, None] == jnp.arange(head_weight.shape[1], dtype=jnp.int32)[None, :]).astype(jnp.float32)
    scale = 1.0 / jnp.sqrt(jnp.float32(height * width))
    dlogits = ((logits - onehot) * scale).astype(jnp.bfloat16)
    dlog_f = dlogits.astype(jnp.float32)
    grad_head = jnp.dot(flat_out.T, dlog_f, precision=lax.Precision.HIGHEST)
    dout_flat = jnp.dot(dlog_f, head_f.T, precision=lax.Precision.HIGHEST) * (flat_out > 0).astype(jnp.float32)
    dout = dout_flat.astype(jnp.bfloat16).reshape(height, width, chans)
    grad_two = kernel_grad(hidden, dout)
    flipped = jnp.transpose(kernel_two[::-1, ::-1], (0, 1, 3, 2))
    dhidden = (convolve(dout, flipped) * (hidden > 0).astype(jnp.float32)).astype(jnp.bfloat16)
    grad_one = kernel_grad(features, dhidden)
    return (section_out, grad_one, grad_two, grad_head)
```

```python
import functools
import math

import jax
import jax.numpy as jnp
from jax import lax
from jax.experimental import pallas as pl
from jax.experimental.pallas import tpu as pltpu
from jax.sharding import PartitionSpec as P

MESH = pl.DeviceIdType.MESH
F32 = jnp.float32
BF16 = jnp.bfloat16
NT = (((1,), (1,)), ((), ()))
TN = (((0,), (0,)), ((), ()))

X_UP, X_DOWN, D_UP, D_DOWN = 0, 1, 2, 3
D_A, E_A = 4, 7
H_A, F_A = 10, 13
H_LOW, H_HIGH, F_LOW, F_HIGH = 16, 19, 22, 25
HEAD_A = 28
FIXED = 31


def merge(block):
    lead, sub, lanes = math.prod(block.shape[:-2]), block.shape[-2], block.shape[-1]
    if sub % 16 == 0:
        return block.reshape(lead * sub, lanes)
    return block.astype(F32).reshape(lead * sub, lanes).astype(BF16)


def shifts(row):
    wide = row.astype(F32)
    width = wide.shape[0]
    at = lax.broadcasted_iota(jnp.int32, wide.shape, 0)
    before = jnp.where(at == 0, 0.0, pltpu.roll(wide, 1, 0)).astype(BF16)
    after = jnp.where(at == width - 1, 0.0, pltpu.roll(wide, width - 1, 0)).astype(BF16)
    return before, after


def body(
    count, scale,
    feat, onehot, k1_hbm, k2_hbm, head,
    out, g1_out, g2_out, gh_out,
    x, x3, k1, k2, h4, ft, ht, fq, hq, l3, dq, eq, dlow, dhigh, db, d4,
    g1, g2, r1, r2, acc, gh, ghm, ghz,
    send, recv, local,
):
    width, chans = feat.shape[1], feat.shape[2]
    quads = count // 4
    part = chans // count
    me = lax.axis_index("row")
    p, q = me % 4, me // 4
    mate = {1: p + 1 - 2 * (p % 2), 2: (p + 2) % 4, 3: 3 - p}
    has_low, has_high = me > 0, me < count - 1

    def remote(src, dst, slot, row):
        return pltpu.make_async_remote_copy(
            src_ref=src, dst_ref=dst, send_sem=send.at[slot], recv_sem=recv.at[slot],
            device_id={"row": row}, device_id_type=MESH,
        )

    load_x = pltpu.make_async_copy(feat, x.at[pl.ds(2, 2)], local.at[0])
    load_k1 = pltpu.make_async_copy(k1_hbm, k1, local.at[1])
    load_k2 = pltpu.make_async_copy(k2_hbm, k2, local.at[2])
    load_x.start()
    load_k1.start()
    load_k2.start()

    barrier = pltpu.get_barrier_semaphore()

    def greet(row):
        pl.semaphore_signal(barrier, inc=1, device_id={"row": row}, device_id_type=MESH)

    for k in (1, 2, 3):
        greet(4 * q + mate[k])
    for k in range(1, quads):
        greet(4 * ((q + k) % quads) + p)

    @pl.when(has_low)
    def _():
        greet(me - 1)

    @pl.when(has_high)
    def _():
        greet(me + 1)

    sides = (me + count - 1) // count + (2 * count - 2 - me) // count
    pl.semaphore_wait(barrier, quads + 2 + sides)

    x_up = remote(feat, x.at[pl.ds(0, 2)], X_UP, me + 1)
    x_down = remote(feat, x.at[pl.ds(4, 2)], X_DOWN, me - 1)

    @pl.when(has_high)
    def _():
        x_up.start()

    @pl.when(has_low)
    def _():
        x_down.start()

    def fill_x3(row, value):
        before, after = shifts(value)
        rows = pl.ds(row * width, width)
        x3[rows, 0:chans] = before
        x3[rows, chans : 2 * chans] = value
        x3[rows, 2 * chans : 3 * chans] = after

    load_x.wait()
    fill_x3(2, x[2])
    fill_x3(3, x[3])

    @pl.when(has_low)
    def _():
        x_up.wait_recv()

    @pl.when(jnp.logical_not(has_low))
    def _():
        x[0:2] = jnp.zeros((2, width, chans), BF16)

    fill_x3(0, x[0])
    fill_x3(1, x[1])

    @pl.when(has_high)
    def _():
        x_down.wait_recv()

    @pl.when(jnp.logical_not(has_high))
    def _():
        x[4:6] = jnp.zeros((2, width, chans), BF16)

    fill_x3(4, x[4])
    fill_x3(5, x[5])

    def conv(rows, kernel):
        size = rows * width
        for a in range(3):
            term = jnp.dot(
                x3[a * width : a * width + size, :],
                kernel[a].reshape(3 * chans, chans),
                preferred_element_type=F32,
            )
            if a == 0:
                acc[0:size, :] = term
            else:
                acc[0:size, :] += term

    load_k1.wait()
    conv(4, k1)
    for row in range(4):
        value = jnp.maximum(acc[row * width : (row + 1) * width, :], 0.0)
        if row == 0:
            value = value * has_low.astype(F32)
        if row == 3:
            value = value * has_high.astype(F32)
        h4[row] = value.astype(BF16)

    def transpose_rows(source, first, target):
        for row in range(4):
            flipped = jnp.transpose(source[first + row].astype(F32))
            target[row] = flipped.reshape(quads, 4, part, width).astype(BF16)

    def spread(source, target, slot, low_slot, high_slot, sem):
        own = pltpu.make_async_copy(
            source.at[pl.ds(1, 2), :, p], target.at[pl.ds(1 + 2 * p, 2)], local.at[sem]
        )
        own.start()
        mids, lows, highs = [], [], []
        for k in (1, 2, 3):
            mids.append(remote(
                source.at[pl.ds(1, 2), :, mate[k]], target.at[pl.ds(1 + 2 * p, 2)],
                slot + k - 1, 4 * q + mate[k],
            ))
            lows.append(remote(
                source.at[pl.ds(0, 1), :, mate[k]], target.at[pl.ds(0, 1)],
                low_slot + k - 1, 4 * q + mate[k],
            ))
            highs.append(remote(
                source.at[pl.ds(3, 1), :, mate[k]], target.at[pl.ds(9, 1)],
                high_slot + k - 1, 4 * q + mate[k],
            ))
        low_own = pltpu.make_async_copy(
            source.at[pl.ds(0, 1), :, p], target.at[pl.ds(0, 1)], local.at[sem + 1]
        )
        high_own = pltpu.make_async_copy(
            source.at[pl.ds(3, 1), :, p], target.at[pl.ds(9, 1)], local.at[sem + 2]
        )
        for copy in mids:
            copy.start()

        @pl.when(p == 0)
        def _():
            low_own.start()
            for copy in lows:
                copy.start()

        @pl.when(p == 3)
        def _():
            high_own.start()
            for copy in highs:
                copy.start()

        def wait_in():
            own.wait()
            for copy in mids:
                copy.wait_recv()

            @pl.when(p == 0)
            def _():
                low_own.wait()

            @pl.when(p == 3)
            def _():
                high_own.wait()

            for k in (1, 2, 3):
                @pl.when(p == k)
                def _():
                    lows[k - 1].wait_recv()

                @pl.when(p == 3 - k)
                def _():
                    highs[k - 1].wait_recv()

        def wait_out():
            for copy in mids:
                copy.wait_send()

            @pl.when(p == 0)
            def _():
                for copy in lows:
                    copy.wait_send()

            @pl.when(p == 3)
            def _():
                for copy in highs:
                    copy.wait_send()

        return wait_in, wait_out

    transpose_rows(h4, 0, ht)
    h_in, h_sent = spread(ht, hq, H_A, H_LOW, H_HIGH, 3)

    for row in range(4):
        fill_x3(row, h4[row])
    load_k2.wait()
    conv(2, k2)
    section = jnp.maximum(acc[0 : 2 * width, :], 0.0).astype(BF16)
    out[...] = section.reshape(2, width, chans)
    logits = lax.dot_general(section, head[...], NT, preferred_element_type=F32)
    dlogits = ((logits - onehot[...]) * scale).astype(BF16)
    dout = jnp.dot(dlogits, head[...], preferred_element_type=F32)
    dout = jnp.where(section.astype(F32) > 0, dout, 0.0).astype(BF16)
    mine = pl.ds(2 * p, 2)
    dq[mine] = dout.reshape(2, width, chans)

    d_up = remote(dq.at[pl.ds(2 * p + 1, 1)], dlow, D_UP, me + 1)
    d_down = remote(dq.at[pl.ds(2 * p, 1)], dhigh, D_DOWN, me - 1)

    @pl.when(has_high)
    def _():
        d_up.start()

    @pl.when(has_low)
    def _():
        d_down.start()

    def gather(buffer, slot):
        near = remote(buffer.at[mine], buffer.at[mine], slot, 4 * q + mate[1])
        far = remote(buffer.at[mine], buffer.at[mine], slot + 1, 4 * q + mate[2])
        theirs = pl.ds(2 * mate[2], 2)
        passed = remote(buffer.at[theirs], buffer.at[theirs], slot + 2, 4 * q + mate[1])
        far.start()
        near.start()
        return near, far, passed

    d_near, d_far, d_passed = gather(dq, D_A)

    gh[...] = lax.dot_general(dlogits, section, TN, preferred_element_type=F32)
    heads = []
    for k in (1, 2, 3):
        copy = remote(gh, ghm.at[k - 1], HEAD_A + k - 1, 4 * q + mate[k])
        copy.start()
        heads.append(copy)
    transpose_rows(x, 1, ft)
    f_in, f_sent = spread(ft, fq, F_A, F_LOW, F_HIGH, 6)

    def fill_d4(row, value):
        before, after = shifts(value)
        rows = pl.ds(row * width, width)
        d4[0, rows, :] = after
        d4[1, rows, :] = value
        d4[2, rows, :] = before

    fill_d4(1, dq[2 * p])
    fill_d4(2, dq[2 * p + 1])

    @pl.when(has_low)
    def _():
        d_up.wait_recv()

    @pl.when(jnp.logical_not(has_low))
    def _():
        dlow[...] = jnp.zeros((1, width, chans), BF16)

    fill_d4(0, dlow[0])

    @pl.when(has_high)
    def _():
        d_down.wait_recv()

    @pl.when(jnp.logical_not(has_high))
    def _():
        dhigh[...] = jnp.zeros((1, width, chans), BF16)

    fill_d4(3, dhigh[0])

    two = 2 * width
    for a in range(3):
        for b in range(3):
            term = lax.dot_general(
                d4[b, (2 - a) * width : (2 - a) * width + two, :], k2[a, b], NT,
                preferred_element_type=F32,
            )
            if a == 0 and b == 0:
                acc[0:two, :] = term
            else:
                acc[0:two, :] += term
    hidden = h4[1:3].reshape(two, chans).astype(F32)
    dhidden = jnp.where(hidden > 0, acc[0:two, :], 0.0).astype(BF16)
    eq[mine] = dhidden.reshape(2, width, chans)
    e_near, e_far, e_passed = gather(eq, E_A)

    def fill_l3(source):
        for row in range(8):
            l3[:, row * width : (row + 1) * width] = merge(source[row : row + 3])

    def fill_db(buffer, block):
        for row in range(2):
            before, after = shifts(buffer[2 * block + row])
            rows = pl.ds(pl.multiple_of((2 * block + row) * width, width), width)
            db[0, rows, :] = after
            db[1, rows, :] = before

    def kernel_grad(buffer, target):
        for b in range(3):
            if b == 1:
                rhs = buffer[...].reshape(8 * width, chans)
            else:
                rhs = db[b // 2]
            term = jnp.dot(l3[...], rhs, preferred_element_type=F32)
            term = term.reshape(3, quads, part, chans)
            for other in range(quads):
                target[other, :, b] = term[:, other].astype(BF16)

    def scatter(source, landing, slot):
        copies = []
        for k in range(1, quads):
            other = (q + k) % quads
            copy = remote(source.at[other], landing.at[k - 1], slot + k - 1, 4 * other + p)
            copy.start()
            copies.append(copy)
        return copies

    def grad_stage(spread_in, source, copies, buffer, target, landing, slot):
        near, far, passed = copies
        fill_db(buffer, p)
        far.wait_recv()
        passed.start()
        spread_in()
        fill_l3(source)
        near.wait_recv()
        fill_db(buffer, mate[1])
        fill_db(buffer, mate[2])
        passed.wait_recv()
        fill_db(buffer, mate[3])
        kernel_grad(buffer, target)
        return scatter(target, landing, slot)

    s2 = grad_stage(h_in, hq, (d_near, d_far, d_passed), dq, g2, r2, FIXED)
    s1 = grad_stage(f_in, fq, (e_near, e_far, e_passed), eq, g1, r1, FIXED + quads - 1)

    for copy in heads:
        copy.wait_recv()
        copy.wait_send()
    gh[...] = gh[...] + ghm[0] + ghm[1] + ghm[2]
    zs = []
    for k in range(1, quads):
        copy = remote(
            gh, ghz.at[k - 1], FIXED + 2 * (quads - 1) + k - 1, 4 * ((q + k) % quads) + p
        )
        copy.start()
        zs.append(copy)

    def finish(copies, source, landing, target):
        for copy in copies:
            copy.wait_recv()
        for a in range(3):
            total = source[q, a].astype(F32)
            for k in range(quads - 1):
                total = total + landing[k, a].astype(F32)
            target[a] = total

    finish(s2, g2, r2, g2_out)
    total = gh[...]
    for k, copy in enumerate(zs):
        copy.wait_recv()
        total = total + ghz[k]
    gh_out[...] = total
    finish(s1, g1, r1, g1_out)

    @pl.when(has_high)
    def _():
        x_up.wait_send()
        d_up.wait_send()

    @pl.when(has_low)
    def _():
        x_down.wait_send()
        d_down.wait_send()

    h_sent()
    f_sent()
    for copy in (d_near, d_far, d_passed, e_near, e_far, e_passed, *s1, *s2, *zs):
        copy.wait_send()


def per_device(features, labels, kernel_one, kernel_two, head_weight):
    rows, width, chans = features.shape
    classes = head_weight.shape[1]
    count = lax.axis_size("row")
    quads, part = count // 4, chans // count
    scale = 1.0 / math.sqrt(rows * count * width)
    onehot = (labels.reshape(-1)[:, None] == jnp.arange(classes, dtype=jnp.int32)[None, :]).astype(
        F32
    )
    slots = FIXED + 3 * (quads - 1)
    vmem = pl.BlockSpec(memory_space=pltpu.VMEM)
    hbm = pl.BlockSpec(memory_space=pl.ANY)
    scratch = [
        pltpu.VMEM((6, width, chans), BF16),
        pltpu.VMEM((6 * width, 3 * chans), BF16),
        pltpu.VMEM((3, 3, chans, chans), BF16),
        pltpu.VMEM((3, 3, chans, chans), BF16),
        pltpu.VMEM((4, width, chans), BF16),
        pltpu.VMEM((4, quads, 4, part, width), BF16),
        pltpu.VMEM((4, quads, 4, part, width), BF16),
        pltpu.VMEM((10, quads, part, width), BF16),
        pltpu.VMEM((10, quads, part, width), BF16),
        pltpu.VMEM((3 * quads * part, 8 * width), BF16),
        pltpu.VMEM((8, width, chans), BF16),
        pltpu.VMEM((8, width, chans), BF16),
        pltpu.VMEM((1, width, chans), BF16),
        pltpu.VMEM((1, width, chans), BF16),
        pltpu.VMEM((2, 8 * width, chans), BF16),
        pltpu.VMEM((3, 4 * width, chans), BF16),
        pltpu.VMEM((quads, 3, 3, part, chans), BF16),
        pltpu.VMEM((quads, 3, 3, part, chans), BF16),
        pltpu.VMEM((quads - 1, 3, 3, part, chans), BF16),
        pltpu.VMEM((quads - 1, 3, 3, part, chans), BF16),
        pltpu.VMEM((4 * width, chans), F32),
        pltpu.VMEM((classes, chans), F32),
        pltpu.VMEM((3, classes, chans), F32),
        pltpu.VMEM((quads - 1, classes, chans), F32),
        pltpu.SemaphoreType.DMA((slots,)),
        pltpu.SemaphoreType.DMA((slots,)),
        pltpu.SemaphoreType.DMA((9,)),
    ]
    section_out, one, two, head_t = pl.pallas_call(
        functools.partial(body, count, scale),
        out_shape=(
            jax.ShapeDtypeStruct((rows, width, chans), BF16),
            jax.ShapeDtypeStruct((3, 3, part, chans), F32),
            jax.ShapeDtypeStruct((3, 3, part, chans), F32),
            jax.ShapeDtypeStruct((classes, chans), F32),
        ),
        in_specs=[hbm, vmem, hbm, hbm, vmem],
        out_specs=(vmem, vmem, vmem, vmem),
        scratch_shapes=scratch,
        compiler_params=pltpu.CompilerParams(
            collective_id=0, has_side_effects=True, vmem_limit_bytes=60 * 2**20
        ),
    )(features, onehot, kernel_one, kernel_two, head_weight.T)
    head_block = lax.dynamic_slice_in_dim(head_t, lax.axis_index("row") * part, part, axis=1)
    return (
        section_out,
        jnp.transpose(one, (2, 0, 1, 3)),
        jnp.transpose(two, (2, 0, 1, 3)),
        head_block.T,
    )


def solution(mesh):
    placed = (P(("groups", "row"), None, None), P(("groups", "row"), None), P(), P(), P())
    return jax.shard_map(
        per_device,
        mesh=mesh,
        in_specs=placed,
        out_specs=(
            P(("groups", "row"), None, None),
            P(("groups", "row"), None, None, None),
            P(("groups", "row"), None, None, None),
            P(("groups", "row"), None),
        ),
        check_vma=False,
    )
```

```python
import functools
import math

import jax
import jax.numpy as jnp
from jax import lax
from jax.experimental import pallas as pl
from jax.experimental.pallas import tpu as pltpu
from jax.sharding import PartitionSpec as P

MESH = pl.DeviceIdType.MESH
F32 = jnp.float32
BF16 = jnp.bfloat16
NT = (((1,), (1,)), ((), ()))
TN = (((0,), (0,)), ((), ()))

X_UP, X_DOWN, D_UP, D_DOWN = 0, 1, 2, 3
D_A, E_A = 4, 7
H_A, F_A = 10, 13
H_LOW, H_HIGH, F_LOW, F_HIGH = 16, 19, 22, 25
HEAD_A = 28
FIXED = 31


def merge(block):
    lead, sub, lanes = math.prod(block.shape[:-2]), block.shape[-2], block.shape[-1]
    if sub % 16 == 0:
        return block.reshape(lead * sub, lanes)
    return block.astype(F32).reshape(lead * sub, lanes).astype(BF16)


def shifts(row):
    wide = row.astype(F32)
    width = wide.shape[0]
    at = lax.broadcasted_iota(jnp.int32, wide.shape, 0)
    before = jnp.where(at == 0, 0.0, pltpu.roll(wide, 1, 0)).astype(BF16)
    after = jnp.where(at == width - 1, 0.0, pltpu.roll(wide, width - 1, 0)).astype(BF16)
    return before, after


def body(
    count, scale,
    feat, onehot, k1_hbm, k2_hbm, head,
    out, g1_out, g2_out, gh_out,
    x, x3, k1, k2, h4, ft, ht, fq, hq, l3, dq, eq, dlow, dhigh, db, d4,
    g1, g2, m1, m2, c1, c2, r1, r2, acc, gh, ghm, ghz,
    send, recv, local,
):
    width, chans = feat.shape[1], feat.shape[2]
    quads = count // 4
    part = chans // count
    me = lax.axis_index("row")
    p, q = me % 4, me // 4
    mate = {1: p + 1 - 2 * (p % 2), 2: (p + 2) % 4, 3: 3 - p}
    has_low, has_high = me > 0, me < count - 1

    def remote(src, dst, slot, row):
        return pltpu.make_async_remote_copy(
            src_ref=src, dst_ref=dst, send_sem=send.at[slot], recv_sem=recv.at[slot],
            device_id={"row": row}, device_id_type=MESH,
        )

    load_x = pltpu.make_async_copy(feat, x.at[pl.ds(2, 2)], local.at[0])
    load_k1 = pltpu.make_async_copy(k1_hbm, k1, local.at[1])
    load_k2 = pltpu.make_async_copy(k2_hbm, k2, local.at[2])
    load_x.start()
    load_k1.start()
    load_k2.start()

    barrier = pltpu.get_barrier_semaphore()

    def greet(row):
        pl.semaphore_signal(barrier, inc=1, device_id={"row": row}, device_id_type=MESH)

    for k in (1, 2, 3):
        greet(4 * q + mate[k])
    for k in range(1, quads):
        greet(4 * ((q + k) % quads) + p)

    @pl.when(has_low)
    def _():
        greet(me - 1)

    @pl.when(has_high)
    def _():
        greet(me + 1)

    sides = (me + count - 1) // count + (2 * count - 2 - me) // count
    pl.semaphore_wait(barrier, quads + 2 + sides)

    x_up = remote(feat, x.at[pl.ds(0, 2)], X_UP, me + 1)
    x_down = remote(feat, x.at[pl.ds(4, 2)], X_DOWN, me - 1)

    @pl.when(has_high)
    def _():
        x_up.start()

    @pl.when(has_low)
    def _():
        x_down.start()

    def fill_x3(row, value):
        before, after = shifts(value)
        rows = pl.ds(row * width, width)
        x3[rows, 0:chans] = before
        x3[rows, chans : 2 * chans] = value
        x3[rows, 2 * chans : 3 * chans] = after

    load_x.wait()
    fill_x3(2, x[2])
    fill_x3(3, x[3])

    @pl.when(has_low)
    def _():
        x_up.wait_recv()

    @pl.when(jnp.logical_not(has_low))
    def _():
        x[0:2] = jnp.zeros((2, width, chans), BF16)

    fill_x3(0, x[0])
    fill_x3(1, x[1])

    @pl.when(has_high)
    def _():
        x_down.wait_recv()

    @pl.when(jnp.logical_not(has_high))
    def _():
        x[4:6] = jnp.zeros((2, width, chans), BF16)

    fill_x3(4, x[4])
    fill_x3(5, x[5])

    def conv(rows, kernel):
        size = rows * width
        for a in range(3):
            term = jnp.dot(
                x3[a * width : a * width + size, :],
                kernel[a].reshape(3 * chans, chans),
                preferred_element_type=F32,
            )
            if a == 0:
                acc[0:size, :] = term
            else:
                acc[0:size, :] += term

    load_k1.wait()
    conv(4, k1)
    for row in range(4):
        value = jnp.maximum(acc[row * width : (row + 1) * width, :], 0.0)
        if row == 0:
            value = value * has_low.astype(F32)
        if row == 3:
            value = value * has_high.astype(F32)
        h4[row] = value.astype(BF16)

    def transpose_rows(source, first, target):
        for row in range(4):
            flipped = jnp.transpose(source[first + row].astype(F32))
            target[row] = flipped.reshape(quads, 4, part, width).astype(BF16)

    def spread(source, target, slot, low_slot, high_slot, sem):
        own = pltpu.make_async_copy(
            source.at[pl.ds(1, 2), :, p], target.at[pl.ds(1 + 2 * p, 2)], local.at[sem]
        )
        own.start()
        mids, lows, highs = [], [], []
        for k in (1, 2, 3):
            mids.append(remote(
                source.at[pl.ds(1, 2), :, mate[k]], target.at[pl.ds(1 + 2 * p, 2)],
                slot + k - 1, 4 * q + mate[k],
            ))
            lows.append(remote(
                source.at[pl.ds(0, 1), :, mate[k]], target.at[pl.ds(0, 1)],
                low_slot + k - 1, 4 * q + mate[k],
            ))
            highs.append(remote(
                source.at[pl.ds(3, 1), :, mate[k]], target.at[pl.ds(9, 1)],
                high_slot + k - 1, 4 * q + mate[k],
            ))
        low_own = pltpu.make_async_copy(
            source.at[pl.ds(0, 1), :, p], target.at[pl.ds(0, 1)], local.at[sem + 1]
        )
        high_own = pltpu.make_async_copy(
            source.at[pl.ds(3, 1), :, p], target.at[pl.ds(9, 1)], local.at[sem + 2]
        )
        for copy in mids:
            copy.start()

        @pl.when(p == 0)
        def _():
            low_own.start()
            for copy in lows:
                copy.start()

        @pl.when(p == 3)
        def _():
            high_own.start()
            for copy in highs:
                copy.start()

        def wait_in():
            own.wait()
            for copy in mids:
                copy.wait_recv()

            @pl.when(p == 0)
            def _():
                low_own.wait()

            @pl.when(p == 3)
            def _():
                high_own.wait()

            for k in (1, 2, 3):
                @pl.when(p == k)
                def _():
                    lows[k - 1].wait_recv()

                @pl.when(p == 3 - k)
                def _():
                    highs[k - 1].wait_recv()

        def wait_out():
            for copy in mids:
                copy.wait_send()

            @pl.when(p == 0)
            def _():
                for copy in lows:
                    copy.wait_send()

            @pl.when(p == 3)
            def _():
                for copy in highs:
                    copy.wait_send()

        return wait_in, wait_out

    transpose_rows(h4, 0, ht)
    h_in, h_sent = spread(ht, hq, H_A, H_LOW, H_HIGH, 3)

    for row in range(4):
        fill_x3(row, h4[row])
    load_k2.wait()
    conv(2, k2)
    section = jnp.maximum(acc[0 : 2 * width, :], 0.0).astype(BF16)
    out[...] = section.reshape(2, width, chans)
    logits = lax.dot_general(section, head[...], NT, preferred_element_type=F32)
    dlogits = ((logits - onehot[...]) * scale).astype(BF16)
    dout = jnp.dot(dlogits, head[...], preferred_element_type=F32)
    dout = jnp.where(section.astype(F32) > 0, dout, 0.0).astype(BF16)
    mine = pl.ds(2 * p, 2)
    dq[mine] = dout.reshape(2, width, chans)

    d_up = remote(dq.at[pl.ds(2 * p + 1, 1)], dlow, D_UP, me + 1)
    d_down = remote(dq.at[pl.ds(2 * p, 1)], dhigh, D_DOWN, me - 1)

    @pl.when(has_high)
    def _():
        d_up.start()

    @pl.when(has_low)
    def _():
        d_down.start()

    def gather(buffer, slot):
        near = remote(buffer.at[mine], buffer.at[mine], slot, 4 * q + mate[1])
        far = remote(buffer.at[mine], buffer.at[mine], slot + 1, 4 * q + mate[2])
        theirs = pl.ds(2 * mate[2], 2)
        passed = remote(buffer.at[theirs], buffer.at[theirs], slot + 2, 4 * q + mate[1])
        far.start()
        near.start()
        return near, far, passed

    d_near, d_far, d_passed = gather(dq, D_A)

    gh[...] = lax.dot_general(dlogits, section, TN, preferred_element_type=F32)
    heads = []
    for k in (1, 2, 3):
        copy = remote(gh, ghm.at[k - 1], HEAD_A + k - 1, 4 * q + mate[k])
        copy.start()
        heads.append(copy)
    transpose_rows(x, 1, ft)
    f_in, f_sent = spread(ft, fq, F_A, F_LOW, F_HIGH, 6)

    def fill_d4(row, value):
        before, after = shifts(value)
        rows = pl.ds(row * width, width)
        d4[0, rows, :] = after
        d4[1, rows, :] = value
        d4[2, rows, :] = before

    fill_d4(1, dq[2 * p])
    fill_d4(2, dq[2 * p + 1])

    @pl.when(has_low)
    def _():
        d_up.wait_recv()

    @pl.when(jnp.logical_not(has_low))
    def _():
        dlow[...] = jnp.zeros((1, width, chans), BF16)

    fill_d4(0, dlow[0])

    @pl.when(has_high)
    def _():
        d_down.wait_recv()

    @pl.when(jnp.logical_not(has_high))
    def _():
        dhigh[...] = jnp.zeros((1, width, chans), BF16)

    fill_d4(3, dhigh[0])

    two = 2 * width
    for a in range(3):
        for b in range(3):
            term = lax.dot_general(
                d4[b, (2 - a) * width : (2 - a) * width + two, :], k2[a, b], NT,
                preferred_element_type=F32,
            )
            if a == 0 and b == 0:
                acc[0:two, :] = term
            else:
                acc[0:two, :] += term
    hidden = h4[1:3].reshape(two, chans).astype(F32)
    dhidden = jnp.where(hidden > 0, acc[0:two, :], 0.0).astype(BF16)
    eq[mine] = dhidden.reshape(2, width, chans)
    e_near, e_far, e_passed = gather(eq, E_A)

    def fill_l3(source):
        for row in range(8):
            l3[:, row * width : (row + 1) * width] = merge(source[row : row + 3])

    def fill_db(buffer, block):
        for row in range(2):
            before, after = shifts(buffer[2 * block + row])
            rows = pl.ds(pl.multiple_of((2 * block + row) * width, width), width)
            db[0, rows, :] = after
            db[1, rows, :] = before

    half = quads // 2
    side, pair = q % 2, q // 2
    twin = 4 * (q + 1 - 2 * side) + p

    def kernel_grad(buffer, target, met, slot):
        copies = []
        for b in range(3):
            if b == 1:
                rhs = buffer[...].reshape(8 * width, chans)
            else:
                rhs = db[b // 2]
            term = jnp.dot(l3[...], rhs, preferred_element_type=F32)
            term = term.reshape(3, quads, part, chans)
            for other in range(quads):
                target[other % 2, other // 2, b] = term[:, other].astype(BF16)
            copy = remote(target.at[1 - side, :, b], met.at[b], slot + b, twin)
            copy.start()
            copies.append(copy)
        return copies

    def combine(copies, target, met, joined, landing, slot):
        sent = []
        for b in range(3):
            copies[b].wait_recv()
            for other in range(half):
                total = target[side, other, b].astype(F32) + met[b, other].astype(F32)
                joined[b, other] = total.astype(BF16)
            for k in range(1, half):
                goal = (pair + k) % half
                copy = remote(
                    joined.at[b, goal], landing.at[k - 1, b],
                    slot + 3 + 3 * (k - 1) + b, 4 * (2 * goal + side) + p,
                )
                copy.start()
                sent.append(copy)
        return sent

    def grad_stage(spread_in, source, copies, buffer, target, met, slot):
        near, far, passed = copies
        fill_db(buffer, p)
        far.wait_recv()
        passed.start()
        spread_in()
        fill_l3(source)
        near.wait_recv()
        fill_db(buffer, mate[1])
        fill_db(buffer, mate[2])
        passed.wait_recv()
        fill_db(buffer, mate[3])
        return kernel_grad(buffer, target, met, slot)

    per_grad = 3 * half
    m2_copies = grad_stage(h_in, hq, (d_near, d_far, d_passed), dq, g2, m2, FIXED)
    m1_copies = grad_stage(f_in, fq, (e_near, e_far, e_passed), eq, g1, m1, FIXED + per_grad)
    s2 = combine(m2_copies, g2, m2, c2, r2, FIXED)
    s1 = combine(m1_copies, g1, m1, c1, r1, FIXED + per_grad)

    for copy in heads:
        copy.wait_recv()
        copy.wait_send()
    gh[...] = gh[...] + ghm[0] + ghm[1] + ghm[2]
    zs = []
    for k in range(1, quads):
        copy = remote(
            gh, ghz.at[k - 1], FIXED + 2 * per_grad + k - 1, 4 * ((q + k) % quads) + p
        )
        copy.start()
        zs.append(copy)

    def finish(copies, source, met, landing, target):
        for copy in copies:
            copy.wait_recv()
        for b in range(3):
            total = source[side, pair, b].astype(F32) + met[b, pair].astype(F32)
            for k in range(half - 1):
                total = total + landing[k, b].astype(F32)
            target[:, b] = total

    finish(s2, g2, m2, r2, g2_out)
    total = gh[...]
    for k, copy in enumerate(zs):
        copy.wait_recv()
        total = total + ghz[k]
    gh_out[...] = total
    finish(s1, g1, m1, r1, g1_out)

    @pl.when(has_high)
    def _():
        x_up.wait_send()
        d_up.wait_send()

    @pl.when(has_low)
    def _():
        x_down.wait_send()
        d_down.wait_send()

    h_sent()
    f_sent()
    for copy in (d_near, d_far, d_passed, e_near, e_far, e_passed, *s1, *s2, *zs, *m1_copies, *m2_copies):
        copy.wait_send()


def per_device(features, labels, kernel_one, kernel_two, head_weight):
    rows, width, chans = features.shape
    classes = head_weight.shape[1]
    count = lax.axis_size("row")
    quads, part = count // 4, chans // count
    scale = 1.0 / math.sqrt(rows * count * width)
    onehot = (labels.reshape(-1)[:, None] == jnp.arange(classes, dtype=jnp.int32)[None, :]).astype(
        F32
    )
    slots = FIXED + 3 * quads + quads - 1
    vmem = pl.BlockSpec(memory_space=pltpu.VMEM)
    hbm = pl.BlockSpec(memory_space=pl.ANY)
    scratch = [
        pltpu.VMEM((6, width, chans), BF16),
        pltpu.VMEM((6 * width, 3 * chans), BF16),
        pltpu.VMEM((3, 3, chans, chans), BF16),
        pltpu.VMEM((3, 3, chans, chans), BF16),
        pltpu.VMEM((4, width, chans), BF16),
        pltpu.VMEM((4, quads, 4, part, width), BF16),
        pltpu.VMEM((4, quads, 4, part, width), BF16),
        pltpu.VMEM((10, quads, part, width), BF16),
        pltpu.VMEM((10, quads, part, width), BF16),
        pltpu.VMEM((3 * quads * part, 8 * width), BF16),
        pltpu.VMEM((8, width, chans), BF16),
        pltpu.VMEM((8, width, chans), BF16),
        pltpu.VMEM((1, width, chans), BF16),
        pltpu.VMEM((1, width, chans), BF16),
        pltpu.VMEM((2, 8 * width, chans), BF16),
        pltpu.VMEM((3, 4 * width, chans), BF16),
        pltpu.VMEM((2, quads // 2, 3, 3, part, chans), BF16),
        pltpu.VMEM((2, quads // 2, 3, 3, part, chans), BF16),
        pltpu.VMEM((3, quads // 2, 3, part, chans), BF16),
        pltpu.VMEM((3, quads // 2, 3, part, chans), BF16),
        pltpu.VMEM((3, quads // 2, 3, part, chans), BF16),
        pltpu.VMEM((3, quads // 2, 3, part, chans), BF16),
        pltpu.VMEM((quads // 2 - 1, 3, 3, part, chans), BF16),
        pltpu.VMEM((quads // 2 - 1, 3, 3, part, chans), BF16),
        pltpu.VMEM((4 * width, chans), F32),
        pltpu.VMEM((classes, chans), F32),
        pltpu.VMEM((3, classes, chans), F32),
        pltpu.VMEM((quads - 1, classes, chans), F32),
        pltpu.SemaphoreType.DMA((slots,)),
        pltpu.SemaphoreType.DMA((slots,)),
        pltpu.SemaphoreType.DMA((9,)),
    ]
    section_out, one, two, head_t = pl.pallas_call(
        functools.partial(body, count, scale),
        out_shape=(
            jax.ShapeDtypeStruct((rows, width, chans), BF16),
            jax.ShapeDtypeStruct((3, 3, part, chans), F32),
            jax.ShapeDtypeStruct((3, 3, part, chans), F32),
            jax.ShapeDtypeStruct((classes, chans), F32),
        ),
        in_specs=[hbm, vmem, hbm, hbm, vmem],
        out_specs=(vmem, vmem, vmem, vmem),
        scratch_shapes=scratch,
        compiler_params=pltpu.CompilerParams(
            collective_id=0, has_side_effects=True, vmem_limit_bytes=60 * 2**20
        ),
    )(features, onehot, kernel_one, kernel_two, head_weight.T)
    head_block = lax.dynamic_slice_in_dim(head_t, lax.axis_index("row") * part, part, axis=1)
    return (
        section_out,
        jnp.transpose(one, (2, 0, 1, 3)),
        jnp.transpose(two, (2, 0, 1, 3)),
        head_block.T,
    )


def solution(mesh):
    placed = (P(("groups", "row"), None, None), P(("groups", "row"), None), P(), P(), P())
    return jax.shard_map(
        per_device,
        mesh=mesh,
        in_specs=placed,
        out_specs=(
            P(("groups", "row"), None, None),
            P(("groups", "row"), None, None, None),
            P(("groups", "row"), None, None, None),
            P(("groups", "row"), None),
        ),
        check_vma=False,
    )
```

```python
import functools
import math

import jax
import jax.numpy as jnp
from jax import lax
from jax.experimental import pallas as pl
from jax.experimental.pallas import tpu as pltpu
from jax.sharding import PartitionSpec as P

MESH = pl.DeviceIdType.MESH
F32 = jnp.float32
BF16 = jnp.bfloat16
NT = (((1,), (1,)), ((), ()))
TN = (((0,), (0,)), ((), ()))

X_UP, X_DOWN, D_UP, D_DOWN = 0, 1, 2, 3
D_A, E_A = 4, 7
H_A, F_A = 10, 13
H_LOW, H_HIGH, F_LOW, F_HIGH = 16, 19, 22, 25
HEAD_A = 28
FIXED = 31


def merge(block):
    lead, sub, lanes = math.prod(block.shape[:-2]), block.shape[-2], block.shape[-1]
    if sub % 16 == 0:
        return block.reshape(lead * sub, lanes)
    return block.astype(F32).reshape(lead * sub, lanes).astype(BF16)


def shifts(row):
    wide = row.astype(F32)
    width = wide.shape[0]
    at = lax.broadcasted_iota(jnp.int32, wide.shape, 0)
    before = jnp.where(at == 0, 0.0, pltpu.roll(wide, 1, 0)).astype(BF16)
    after = jnp.where(at == width - 1, 0.0, pltpu.roll(wide, width - 1, 0)).astype(BF16)
    return before, after


def body(
    count, scale,
    feat, onehot, k1_hbm, k2_hbm, head,
    out, g1_out, g2_out, gh_out,
    x, x3, k1, k2, h4, ft, ht, fq, hq, l3, dq, eq, dlow, dhigh, db, d4,
    g1, g2, m1, m2, c1, c2, r1, r2, acc, gh, ghm, ghz,
    send, recv, local,
):
    width, chans = feat.shape[1], feat.shape[2]
    quads = count // 4
    part = chans // count
    me = lax.axis_index("row")
    p, q = me % 4, me // 4
    mate = {1: p + 1 - 2 * (p % 2), 2: (p + 2) % 4, 3: 3 - p}
    has_low, has_high = me > 0, me < count - 1

    def remote(src, dst, slot, row):
        return pltpu.make_async_remote_copy(
            src_ref=src, dst_ref=dst, send_sem=send.at[slot], recv_sem=recv.at[slot],
            device_id={"row": row}, device_id_type=MESH,
        )

    load_x = pltpu.make_async_copy(feat, x.at[pl.ds(2, 2)], local.at[0])
    load_k1 = pltpu.make_async_copy(k1_hbm, k1, local.at[1])
    load_k2 = pltpu.make_async_copy(k2_hbm, k2, local.at[2])
    load_x.start()
    load_k1.start()
    load_k2.start()

    barrier = pltpu.get_barrier_semaphore()

    def greet(row):
        pl.semaphore_signal(barrier, inc=1, device_id={"row": row}, device_id_type=MESH)

    for k in (1, 2, 3):
        greet(4 * q + mate[k])
    for k in range(1, quads):
        greet(4 * ((q + k) % quads) + p)

    @pl.when(has_low)
    def _():
        greet(me - 1)

    @pl.when(has_high)
    def _():
        greet(me + 1)

    sides = (me + count - 1) // count + (2 * count - 2 - me) // count
    pl.semaphore_wait(barrier, quads + 2 + sides)

    x_up = remote(feat, x.at[pl.ds(0, 2)], X_UP, me + 1)
    x_down = remote(feat, x.at[pl.ds(4, 2)], X_DOWN, me - 1)

    @pl.when(has_high)
    def _():
        x_up.start()

    @pl.when(has_low)
    def _():
        x_down.start()

    def fill_x3(row, value):
        before, after = shifts(value)
        rows = pl.ds(row * width, width)
        x3[rows, 0:chans] = before
        x3[rows, chans : 2 * chans] = value
        x3[rows, 2 * chans : 3 * chans] = after

    load_x.wait()
    fill_x3(2, x[2])
    fill_x3(3, x[3])

    @pl.when(has_low)
    def _():
        x_up.wait_recv()

    @pl.when(jnp.logical_not(has_low))
    def _():
        x[0:2] = jnp.zeros((2, width, chans), BF16)

    fill_x3(0, x[0])
    fill_x3(1, x[1])

    @pl.when(has_high)
    def _():
        x_down.wait_recv()

    @pl.when(jnp.logical_not(has_high))
    def _():
        x[4:6] = jnp.zeros((2, width, chans), BF16)

    fill_x3(4, x[4])
    fill_x3(5, x[5])

    def conv(rows, kernel):
        size = rows * width
        for a in range(3):
            term = jnp.dot(
                x3[a * width : a * width + size, :],
                kernel[a].reshape(3 * chans, chans),
                preferred_element_type=F32,
            )
            if a == 0:
                acc[0:size, :] = term
            else:
                acc[0:size, :] += term

    def transpose_rows(source, first, target):
        for row in range(4):
            flipped = jnp.transpose(source[first + row].astype(F32))
            target[row] = flipped.reshape(quads, 4, part, width).astype(BF16)

    def spread(source, target, slot, low_slot, high_slot, sem):
        own = pltpu.make_async_copy(
            source.at[pl.ds(1, 2), :, p], target.at[pl.ds(1 + 2 * p, 2)], local.at[sem]
        )
        own.start()
        mids, lows, highs = [], [], []
        for k in (1, 2, 3):
            mids.append(remote(
                source.at[pl.ds(1, 2), :, mate[k]], target.at[pl.ds(1 + 2 * p, 2)],
                slot + k - 1, 4 * q + mate[k],
            ))
            lows.append(remote(
                source.at[pl.ds(0, 1), :, mate[k]], target.at[pl.ds(0, 1)],
                low_slot + k - 1, 4 * q + mate[k],
            ))
            highs.append(remote(
                source.at[pl.ds(3, 1), :, mate[k]], target.at[pl.ds(9, 1)],
                high_slot + k - 1, 4 * q + mate[k],
            ))
        low_own = pltpu.make_async_copy(
            source.at[pl.ds(0, 1), :, p], target.at[pl.ds(0, 1)], local.at[sem + 1]
        )
        high_own = pltpu.make_async_copy(
            source.at[pl.ds(3, 1), :, p], target.at[pl.ds(9, 1)], local.at[sem + 2]
        )
        for copy in mids:
            copy.start()

        @pl.when(p == 0)
        def _():
            low_own.start()
            for copy in lows:
                copy.start()

        @pl.when(p == 3)
        def _():
            high_own.start()
            for copy in highs:
                copy.start()

        def wait_in():
            own.wait()
            for copy in mids:
                copy.wait_recv()

            @pl.when(p == 0)
            def _():
                low_own.wait()

            @pl.when(p == 3)
            def _():
                high_own.wait()

            for k in (1, 2, 3):
                @pl.when(p == k)
                def _():
                    lows[k - 1].wait_recv()

                @pl.when(p == 3 - k)
                def _():
                    highs[k - 1].wait_recv()

        def wait_out():
            for copy in mids:
                copy.wait_send()

            @pl.when(p == 0)
            def _():
                for copy in lows:
                    copy.wait_send()

            @pl.when(p == 3)
            def _():
                for copy in highs:
                    copy.wait_send()

        return wait_in, wait_out

    transpose_rows(x, 1, ft)
    f_in, f_sent = spread(ft, fq, F_A, F_LOW, F_HIGH, 6)

    load_k1.wait()
    conv(4, k1)
    for row in range(4):
        value = jnp.maximum(acc[row * width : (row + 1) * width, :], 0.0)
        if row == 0:
            value = value * has_low.astype(F32)
        if row == 3:
            value = value * has_high.astype(F32)
        h4[row] = value.astype(BF16)

    transpose_rows(h4, 0, ht)
    h_in, h_sent = spread(ht, hq, H_A, H_LOW, H_HIGH, 3)

    for row in range(4):
        fill_x3(row, h4[row])
    load_k2.wait()
    conv(2, k2)
    section = jnp.maximum(acc[0 : 2 * width, :], 0.0).astype(BF16)
    out[...] = section.reshape(2, width, chans)
    logits = lax.dot_general(section, head[...], NT, preferred_element_type=F32)
    dlogits = ((logits - onehot[...]) * scale).astype(BF16)
    dout = jnp.dot(dlogits, head[...], preferred_element_type=F32)
    dout = jnp.where(section.astype(F32) > 0, dout, 0.0).astype(BF16)
    mine = pl.ds(2 * p, 2)
    dq[mine] = dout.reshape(2, width, chans)

    d_up = remote(dq.at[pl.ds(2 * p + 1, 1)], dlow, D_UP, me + 1)
    d_down = remote(dq.at[pl.ds(2 * p, 1)], dhigh, D_DOWN, me - 1)

    @pl.when(has_high)
    def _():
        d_up.start()

    @pl.when(has_low)
    def _():
        d_down.start()

    def gather(buffer, slot):
        near = remote(buffer.at[mine], buffer.at[mine], slot, 4 * q + mate[1])
        far = remote(buffer.at[mine], buffer.at[mine], slot + 1, 4 * q + mate[2])
        theirs = pl.ds(2 * mate[2], 2)
        passed = remote(buffer.at[theirs], buffer.at[theirs], slot + 2, 4 * q + mate[1])
        far.start()
        near.start()
        return near, far, passed

    d_near, d_far, d_passed = gather(dq, D_A)

    gh[...] = lax.dot_general(dlogits, section, TN, preferred_element_type=F32)
    heads = []
    for k in (1, 2, 3):
        copy = remote(gh, ghm.at[k - 1], HEAD_A + k - 1, 4 * q + mate[k])
        copy.start()
        heads.append(copy)

    def fill_d4(row, value):
        before, after = shifts(value)
        rows = pl.ds(row * width, width)
        d4[0, rows, :] = after
        d4[1, rows, :] = value
        d4[2, rows, :] = before

    fill_d4(1, dq[2 * p])
    fill_d4(2, dq[2 * p + 1])

    @pl.when(has_low)
    def _():
        d_up.wait_recv()

    @pl.when(jnp.logical_not(has_low))
    def _():
        dlow[...] = jnp.zeros((1, width, chans), BF16)

    fill_d4(0, dlow[0])

    @pl.when(has_high)
    def _():
        d_down.wait_recv()

    @pl.when(jnp.logical_not(has_high))
    def _():
        dhigh[...] = jnp.zeros((1, width, chans), BF16)

    fill_d4(3, dhigh[0])

    two = 2 * width
    for a in range(3):
        for b in range(3):
            term = lax.dot_general(
                d4[b, (2 - a) * width : (2 - a) * width + two, :], k2[a, b], NT,
                preferred_element_type=F32,
            )
            if a == 0 and b == 0:
                acc[0:two, :] = term
            else:
                acc[0:two, :] += term
    hidden = h4[1:3].reshape(two, chans).astype(F32)
    dhidden = jnp.where(hidden > 0, acc[0:two, :], 0.0).astype(BF16)
    eq[mine] = dhidden.reshape(2, width, chans)
    e_near, e_far, e_passed = gather(eq, E_A)

    def fill_l3(source):
        for row in range(8):
            l3[:, row * width : (row + 1) * width] = merge(source[row : row + 3])

    def fill_db(buffer, block):
        for row in range(2):
            before, after = shifts(buffer[2 * block + row])
            rows = pl.ds(pl.multiple_of((2 * block + row) * width, width), width)
            db[0, rows, :] = after
            db[1, rows, :] = before

    half = quads // 2
    side, pair = q % 2, q // 2
    twin = 4 * (q + 1 - 2 * side) + p

    def kernel_grad(buffer, target, met, slot):
        copies = []
        for b in range(3):
            if b == 1:
                rhs = buffer[...].reshape(8 * width, chans)
            else:
                rhs = db[b // 2]
            term = jnp.dot(l3[...], rhs, preferred_element_type=F32)
            term = term.reshape(3, quads, part, chans)
            for other in range(quads):
                target[other % 2, other // 2, b] = term[:, other].astype(BF16)
            copy = remote(target.at[1 - side, :, b], met.at[b], slot + b, twin)
            copy.start()
            copies.append(copy)
        return copies

    def combine(copies, target, met, joined, landing, slot):
        sent = []
        for b in range(3):
            copies[b].wait_recv()
            for other in range(half):
                total = target[side, other, b].astype(F32) + met[b, other].astype(F32)
                joined[b, other] = total.astype(BF16)
            for k in range(1, half):
                goal = (pair + k) % half
                copy = remote(
                    joined.at[b, goal], landing.at[k - 1, b],
                    slot + 3 + 3 * (k - 1) + b, 4 * (2 * goal + side) + p,
                )
                copy.start()
                sent.append(copy)
        return sent

    def grad_stage(spread_in, source, copies, buffer, target, met, slot):
        near, far, passed = copies
        fill_db(buffer, p)
        far.wait_recv()
        passed.start()
        spread_in()
        fill_l3(source)
        near.wait_recv()
        fill_db(buffer, mate[1])
        fill_db(buffer, mate[2])
        passed.wait_recv()
        fill_db(buffer, mate[3])
        return kernel_grad(buffer, target, met, slot)

    per_grad = 3 * half
    m2_copies = grad_stage(h_in, hq, (d_near, d_far, d_passed), dq, g2, m2, FIXED)
    m1_copies = grad_stage(f_in, fq, (e_near, e_far, e_passed), eq, g1, m1, FIXED + per_grad)
    s2 = combine(m2_copies, g2, m2, c2, r2, FIXED)
    s1 = combine(m1_copies, g1, m1, c1, r1, FIXED + per_grad)

    for copy in heads:
        copy.wait_recv()
        copy.wait_send()
    gh[...] = gh[...] + ghm[0] + ghm[1] + ghm[2]
    zs = []
    for k in range(1, quads):
        copy = remote(
            gh, ghz.at[k - 1], FIXED + 2 * per_grad + k - 1, 4 * ((q + k) % quads) + p
        )
        copy.start()
        zs.append(copy)

    def finish(copies, source, met, landing, target):
        for copy in copies:
            copy.wait_recv()
        for b in range(3):
            total = source[side, pair, b].astype(F32) + met[b, pair].astype(F32)
            for k in range(half - 1):
                total = total + landing[k, b].astype(F32)
            target[:, b] = total

    finish(s2, g2, m2, r2, g2_out)
    total = gh[...]
    for k, copy in enumerate(zs):
        copy.wait_recv()
        total = total + ghz[k]
    gh_out[...] = total
    finish(s1, g1, m1, r1, g1_out)

    @pl.when(has_high)
    def _():
        x_up.wait_send()
        d_up.wait_send()

    @pl.when(has_low)
    def _():
        x_down.wait_send()
        d_down.wait_send()

    h_sent()
    f_sent()
    for copy in (d_near, d_far, d_passed, e_near, e_far, e_passed, *s1, *s2, *zs, *m1_copies, *m2_copies):
        copy.wait_send()


def per_device(features, labels, kernel_one, kernel_two, head_weight):
    rows, width, chans = features.shape
    classes = head_weight.shape[1]
    count = lax.axis_size("row")
    quads, part = count // 4, chans // count
    scale = 1.0 / math.sqrt(rows * count * width)
    onehot = (labels.reshape(-1)[:, None] == jnp.arange(classes, dtype=jnp.int32)[None, :]).astype(
        F32
    )
    slots = FIXED + 3 * quads + quads - 1
    vmem = pl.BlockSpec(memory_space=pltpu.VMEM)
    hbm = pl.BlockSpec(memory_space=pl.ANY)
    scratch = [
        pltpu.VMEM((6, width, chans), BF16),
        pltpu.VMEM((6 * width, 3 * chans), BF16),
        pltpu.VMEM((3, 3, chans, chans), BF16),
        pltpu.VMEM((3, 3, chans, chans), BF16),
        pltpu.VMEM((4, width, chans), BF16),
        pltpu.VMEM((4, quads, 4, part, width), BF16),
        pltpu.VMEM((4, quads, 4, part, width), BF16),
        pltpu.VMEM((10, quads, part, width), BF16),
        pltpu.VMEM((10, quads, part, width), BF16),
        pltpu.VMEM((3 * quads * part, 8 * width), BF16),
        pltpu.VMEM((8, width, chans), BF16),
        pltpu.VMEM((8, width, chans), BF16),
        pltpu.VMEM((1, width, chans), BF16),
        pltpu.VMEM((1, width, chans), BF16),
        pltpu.VMEM((2, 8 * width, chans), BF16),
        pltpu.VMEM((3, 4 * width, chans), BF16),
        pltpu.VMEM((2, quads // 2, 3, 3, part, chans), BF16),
        pltpu.VMEM((2, quads // 2, 3, 3, part, chans), BF16),
        pltpu.VMEM((3, quads // 2, 3, part, chans), BF16),
        pltpu.VMEM((3, quads // 2, 3, part, chans), BF16),
        pltpu.VMEM((3, quads // 2, 3, part, chans), BF16),
        pltpu.VMEM((3, quads // 2, 3, part, chans), BF16),
        pltpu.VMEM((quads // 2 - 1, 3, 3, part, chans), BF16),
        pltpu.VMEM((quads // 2 - 1, 3, 3, part, chans), BF16),
        pltpu.VMEM((4 * width, chans), F32),
        pltpu.VMEM((classes, chans), F32),
        pltpu.VMEM((3, classes, chans), F32),
        pltpu.VMEM((quads - 1, classes, chans), F32),
        pltpu.SemaphoreType.DMA((slots,)),
        pltpu.SemaphoreType.DMA((slots,)),
        pltpu.SemaphoreType.DMA((9,)),
    ]
    section_out, one, two, head_t = pl.pallas_call(
        functools.partial(body, count, scale),
        out_shape=(
            jax.ShapeDtypeStruct((rows, width, chans), BF16),
            jax.ShapeDtypeStruct((3, 3, part, chans), F32),
            jax.ShapeDtypeStruct((3, 3, part, chans), F32),
            jax.ShapeDtypeStruct((classes, chans), F32),
        ),
        in_specs=[hbm, vmem, hbm, hbm, vmem],
        out_specs=(vmem, vmem, vmem, vmem),
        scratch_shapes=scratch,
        compiler_params=pltpu.CompilerParams(
            collective_id=0, has_side_effects=True, vmem_limit_bytes=60 * 2**20
        ),
    )(features, onehot, kernel_one, kernel_two, head_weight.T)
    head_block = lax.dynamic_slice_in_dim(head_t, lax.axis_index("row") * part, part, axis=1)
    return (
        jnp.maximum(section_out, 0),
        jnp.transpose(one, (2, 0, 1, 3)),
        jnp.transpose(two, (2, 0, 1, 3)),
        head_block.T,
    )


def solution(mesh):
    placed = (P(("groups", "row"), None, None), P(("groups", "row"), None), P(), P(), P())
    return jax.shard_map(
        per_device,
        mesh=mesh,
        in_specs=placed,
        out_specs=(
            P(("groups", "row"), None, None),
            P(("groups", "row"), None, None, None),
            P(("groups", "row"), None, None, None),
            P(("groups", "row"), None),
        ),
        check_vma=False,
    )
```
